32 devices in a mesh: runs: 2 (over y), ens: 2 (over core), space: 8 (over z, x).
Axes of the slice: x: 2, y: 2, z: 4, core: 2. Of those that a mesh axis runs over, the one named last changes fastest.
Arguments:
- analysis: float32 [8, 8, 64, 3600], P(('runs', 'ens'), None, 'space'), parts along dimension 0, may hold values from -6 to 6
- copy_counts: int32 [8], P('runs'), parts along dimension 0, may hold values from 0 to 3, as said below
- spreading_coefficient: float32 [128, 3600], P(('runs', 'space')), parts along dimension 0, may hold values from 0.04 to 0.2
- component_interaction: float32 [8, 8], replicated, may hold values from -0.3 to 0.3
- ocean_mask: int32 [128, 3600], P(('runs', 'space')), parts along dimension 0, may hold values 0 or 1
- measured_grid_location: int32 [8192], P(('runs', 'space')), parts along dimension 0, may hold values from 0 to 28799
- measured_surface_reading: float32 [8192], P(('runs', 'space')), parts along dimension 0, may hold values from -6 to 6
- measured_inverse_variance: float32 [8192], P(('runs', 'space')), parts along dimension 0, may hold values from 0.3 to 27, as said below
Outputs:
- predicted_ensemble: float32 [8, 8, 64, 3600], P(('runs', 'ens'), None, 'space'), parts along dimension 0
- average_fit_score: float32 [8], P(('runs', 'ens')), parts along dimension 0
The draws below stay inside these ranges and needn't reach their ends.
There are 2 independent parts, one for each index of `runs`. The reference program is written for one: setup_inputs(seed, part) draws one part's arguments, and reference() takes and returns one part's arrays. A program takes and returns all parts, laid end to end along the dimension named above; an argument that names none is the same for every part. Nothing has to cross between parts.
Inputs may be any that keep to these rules, and one draw needn't show every extreme that they name: `copy_counts`: the counts sum to 4; one particle gets exactly 3 copies; the particles of the first ens slot together get a count other than 2. `measured_inverse_variance`: Positive.
All inputs are finite; a program needn't handle non-finite values. No bound on the sum of `ocean_mask` on one device may be relied on, other than what follows from the above.
Results may differ from the reference program's by a relative error of at most 0.00011.
Values sent between devices are 32-bit elements; how exact they have to be, the bound alone decides.
A program may use at most 64 MiB of HBM per device.

```python
import math
import jax
import jax.numpy as jnp
from jax import lax

NLON = 3600
COMP = 8
LAT_DEV = 8
SUBSTEPS = 3
OBS_DEV = 512
PARTICLES = 4
NLAT = 64
NOBS = 4096
N_SPACE = 8


def draw_copy_counts(key, part):
    key = jax.random.fold_in(key, 7)
    order = jax.random.permutation(key, PARTICLES).astype(jnp.int32)
    labels = jnp.arange(PARTICLES, dtype=jnp.int32)
    pattern = jnp.where(labels == 0, PARTICLES - 1, jnp.where(labels == 1, 1, 0)).astype(jnp.int32)
    return jnp.sum((order[:, None] == labels[None, :]).astype(jnp.int32) * pattern[:, None], axis=0).astype(jnp.int32)


def draw_measured_inverse_variance(key, part):
    key = jax.random.fold_in(key, 5)
    ramp = jnp.arange(NOBS, dtype=jnp.float32) / (NOBS - 1)
    base = jnp.exp(jax.random.uniform(key, (NOBS,), jnp.float32, math.log(0.3), math.log(3.0)))
    return base * (1.0 + 2.0 * ramp)


def with_ends(drawn, key, low, high):
    longest = drawn.shape.index(max(drawn.shape))
    spots = []
    for shift in (0, 1):
        where = [jax.random.randint(jax.random.fold_in(key, axis), (), 0, length) for axis, length in enumerate(drawn.shape)]
        where[longest] = (where[longest] + shift) % drawn.shape[longest]
        spots.append(tuple(where))
    return drawn.at[spots[0]].set(low).at[spots[1]].set(high)


def shard_levels(key, shape, cuts, low, top_value):
    loudness = 1.0
    for axis_at, shards_of in cuts:
        heights = jax.random.uniform(jax.random.fold_in(jax.random.fold_in(key, 6), axis_at), (shards_of,), jnp.float32, low / len(cuts), top_value / len(cuts))
        loudness = loudness * jnp.repeat(jnp.exp(heights), shape[axis_at] // shards_of).reshape((-1,) + (1,) * (len(shape) - 1 - axis_at))
    return loudness


def normal_values(key, shape, scale, bound, split=(), kind=jnp.bfloat16):
    drawn = scale * jax.random.normal(key, shape, jnp.float32)
    if split:
        drawn = drawn * shard_levels(key, shape, split, -0.22, 0.18)
    return jnp.clip(drawn, -bound, bound).astype(kind)


def setup_inputs(seed: int = 0, part: int = 0) -> dict:
    seeds = jax.random.split(jax.random.key(seed), 9)
    own_keys = jax.random.split(jax.random.fold_in(seeds[8], part), 9)
    return {
        "analysis": normal_values(own_keys[0], (PARTICLES, COMP, NLAT, NLON), 1.0, 6.0, ((0, 2), (2, 8)), jnp.float32),
        "copy_counts": draw_copy_counts(jax.random.fold_in(jax.random.fold_in(seeds[8], part), 71), part),
        "spreading_coefficient": jnp.clip(jnp.exp(math.log(0.2) - 1.609438 * jax.random.uniform(own_keys[2], (NLAT, NLON), jnp.float32) ** shard_levels(own_keys[2], (NLAT, NLON), ((0, 8),), -0.2, 0.2)), 0.04, 0.2),
        "component_interaction": normal_values(seeds[3], (COMP, COMP), 0.05, 0.3, (), jnp.float32),
        "ocean_mask": with_ends((jax.random.randint(own_keys[4], (NLAT, NLON), 0, 10) < 7).astype(jnp.int32), jax.random.fold_in(own_keys[4], 1), 0, 1),
        "measured_grid_location": with_ends(jax.random.randint(own_keys[5], (NOBS,), 0, LAT_DEV * NLON), jax.random.fold_in(own_keys[5], 1), 0, (LAT_DEV * NLON) - 1).astype(jnp.int32),
        "measured_surface_reading": normal_values(own_keys[6], (NOBS,), 1.0, 6.0, ((0, 8),), jnp.float32),
        "measured_inverse_variance": draw_measured_inverse_variance(jax.random.fold_in(jax.random.fold_in(seeds[8], part), 71), part),
    }


def update(padded, spreading_coefficient, water_grid_flag, component_interaction):
    centre = padded[:, :, 1:-1]
    laplace = padded[:, :, 2:] + padded[:, :, :-2] + jnp.roll(centre, -1, axis=3) + jnp.roll(centre, 1, axis=3) - 4.0 * centre
    mixing = jnp.einsum("ij,pjrc->pirc", component_interaction, centre, precision=lax.Precision.HIGHEST)
    return water_grid_flag * (centre + spreading_coefficient * laplace + mixing)


def reference(analysis, copy_counts, spreading_coefficient, component_interaction, ocean_mask, measured_grid_location, measured_surface_reading, measured_inverse_variance):
    bounds = jnp.cumsum(copy_counts).astype(jnp.int32)
    position = jnp.arange(PARTICLES, dtype=jnp.int32)
    parents = jnp.sum((bounds[None, :] <= position[:, None]).astype(jnp.int32), axis=1)
    current = analysis[parents]
    water_grid_flag = ocean_mask.astype(jnp.float32)
    for substep in range(SUBSTEPS):
        padded = jnp.pad(current, ((0, 0), (0, 0), (1, 1), (0, 0)))
        current = update(padded, spreading_coefficient, water_grid_flag, component_interaction)
    surface = current[:, 0].reshape(PARTICLES, N_SPACE, LAT_DEV * NLON)
    obs_rows = jnp.broadcast_to(measured_grid_location.reshape(1, N_SPACE, OBS_DEV), (PARTICLES, N_SPACE, OBS_DEV)).astype(jnp.int32)
    picked = jnp.take_along_axis(surface, obs_rows, axis=2)
    misfit = picked - measured_surface_reading.reshape(1, N_SPACE, OBS_DEV)
    summed = jnp.sum(measured_inverse_variance.reshape(1, N_SPACE, OBS_DEV) * misfit * misfit, axis=(1, 2))
    return current, -0.5 * summed / NOBS
```

```python
import functools

import jax
import jax.numpy as jnp
from jax import lax
from jax.experimental import pallas as pl
from jax.experimental.pallas import tpu as pltpu
from jax.sharding import PartitionSpec as P

SUBSTEPS = 3
CHUNKS = 4
LANES = 128
MESH = pl.DeviceIdType.MESH


def radix_steps(peers):
    steps, stride = [], 1
    while peers > 1:
        size = 8 if peers % 8 == 0 else (peers if peers < 8 else 2 if peers % 2 == 0 else peers)
        steps.append((stride, size))
        stride, peers = stride * size, peers // size
    return steps


def forecast_kernel(
    peers,
    counts,
    inter,
    analysis,
    coef,
    mask,
    loc,
    reading,
    inv_var,
    out,
    totals,
    raw,
    cand,
    taken,
    edges,
    send,
    north,
    south,
    fields,
    result,
    other,
    wet,
    wcoef,
    surface,
    pair,
    gather,
    load_sem,
    edge_sem,
    cand_sem,
    send_sem,
    recv_sem,
    final_send,
    final_recv,
    store_sem,
    pair_sem,
    sum_send,
    sum_recv,
):
    comp, rows, lon = analysis.shape[1:]
    tiles = wet.shape[1] // LANES
    slots = counts.shape[0]
    per_slot = slots // 2
    tail = lon - (tiles - 1) * LANES
    half = (LANES - tail) // 2
    bounds = [tiles * j // CHUNKS for j in range(CHUNKS + 1)]
    steps = radix_steps(peers)

    e = lax.axis_index("ens")
    me = lax.axis_index("space")
    has_north = me > 0
    has_south = me < peers - 1

    loads = [
        pltpu.make_async_copy(analysis.at[p], raw.at[p], load_sem.at[p]) for p in range(per_slot)
    ]
    for copy in loads:
        copy.start()

    def digit_peers():
        for r, (stride, size) in enumerate(steps):
            digit = lax.rem(me // stride, size)
            for q in range(1, size):
                to = lax.rem(digit + q, size)
                yield r, q, digit, to, me + (to - digit) * stride

    barrier = pltpu.get_barrier_semaphore()
    pl.semaphore_signal(barrier, inc=1, device_id={"ens": 1 - e}, device_id_type=MESH)
    waits = 1
    for r, q, digit, to, dev in digit_peers():
        pl.semaphore_signal(barrier, inc=1, device_id={"space": dev}, device_id_type=MESH)
        waits += 1

    if len(steps) > 1:

        @pl.when(has_north)
        def _():
            pl.semaphore_signal(barrier, inc=1, device_id={"space": me - 1}, device_id_type=MESH)

        @pl.when(has_south)
        def _():
            pl.semaphore_signal(barrier, inc=1, device_id={"space": me + 1}, device_id_type=MESH)

        waits = waits + has_north.astype(jnp.int32) + has_south.astype(jnp.int32)

    def tail_of(load):
        return jnp.concatenate(
            [load(lon - tail, lon), load(0, half), load(lon - (LANES - tail - half), lon)], axis=-1
        )

    def tile_loop(first, last, body):
        def step(k, carry):
            body(k, pl.ds(pl.multiple_of(k * LANES, LANES), LANES))
            return carry

        lax.fori_loop(first, last, step, 0)

    last = pl.ds((tiles - 1) * LANES, LANES)

    def prepare(c, m, at):
        w = m.astype(jnp.float32)
        wet[:, at] = w
        wcoef[:, at] = w * c

    tile_loop(0, tiles - 1, lambda k, at: prepare(coef[:, at], mask[:, at], at))
    prepare(
        tail_of(lambda a, b: coef[:, a:b]),
        tail_of(lambda a, b: mask[:, a:b].astype(jnp.float32)),
        last,
    )
    surface[tiles * rows :, :] = jnp.zeros((surface.shape[0] - tiles * rows, LANES), jnp.float32)

    @pl.when(jnp.logical_not(has_north))
    def _():
        for s in range(SUBSTEPS):
            north[s] = jnp.zeros(north.shape[1:], jnp.float32)

    @pl.when(jnp.logical_not(has_south))
    def _():
        for s in range(SUBSTEPS):
            south[s] = jnp.zeros(south.shape[1:], jnp.float32)

    sums, total = [], 0
    for i in range(slots):
        total = total + counts[i]
        sums.append(total)
    first = sum((v <= 0).astype(jnp.int32) for v in sums)
    final = sum((v <= slots - 1).astype(jnp.int32) for v in sums)
    mine = jnp.where(e == 0, first, final)
    theirs = jnp.where(e == 0, final, first)
    is_own = mine // per_slot == e
    their_row = theirs % per_slot
    own_row = mine % per_slot
    edge_row = jnp.where(is_own, 0, 1)

    for copy in loads:
        copy.wait()

    def pack_edges(p, slot):
        def put(load, at):
            for c in range(comp):
                v = load(c)
                edges[slot, 0, c : c + 1, at] = v[0:1]
                edges[slot, 1, c : c + 1, at] = v[rows - 1 : rows]

        tile_loop(0, tiles - 1, lambda k, at: put(lambda c: raw[p, c, :, at], at))
        put(lambda c: tail_of(lambda a, b: raw[p, c, :, a:b]), last)

    pack_edges(their_row, 2)

    pl.semaphore_wait(barrier, waits)

    edge_copy = pltpu.make_async_remote_copy(
        edges.at[2], edges.at[1], edge_sem.at[0], edge_sem.at[1], {"ens": 1 - e}, MESH
    )
    edge_copy.start()
    for c in range(comp):
        cand[c] = raw[their_row, c]
    cand_copy = pltpu.make_async_remote_copy(
        cand, taken, cand_sem.at[0], cand_sem.at[1], {"ens": 1 - e}, MESH
    )
    cand_copy.start()
    pack_edges(own_row, 0)
    edge_copy.wait()

    def halo_copy(s, side, j):
        at = pl.ds(bounds[j] * LANES, (bounds[j + 1] - bounds[j]) * LANES)
        dst = south if side == 0 else north
        to = me - 1 if side == 0 else me + 1
        return pltpu.make_async_remote_copy(
            send.at[s, side, :, at],
            dst.at[s, :, at],
            send_sem.at[s, side, j],
            recv_sem.at[s, side, j],
            {"space": to},
            MESH,
        )

    def send_halo(s, j):
        @pl.when(has_north)
        def _():
            halo_copy(s, 0, j).start()

        @pl.when(has_south)
        def _():
            halo_copy(s, 1, j).start()

    for j in range(CHUNKS):

        def move(k, at):
            for side in range(2):
                send[0, side, :, at] = edges[edge_row, side, :, at]

        tile_loop(bounds[j], bounds[j + 1], move)
        send_halo(0, j)

    cand_copy.wait()

    def begin(k, at):
        for c in range(comp):
            fields[0, c, :, at] = jnp.where(is_own, raw[own_row, c, :, at], taken[c, :, at])

    tile_loop(0, tiles - 1, begin)
    for c in range(comp):
        fields[0, c, :, last] = tail_of(
            lambda a, b: jnp.where(is_own, raw[own_row, c, :, a:b], taken[c, :, a:b])
        )

    lane = lax.broadcasted_iota(jnp.int32, (rows, LANES), 1)
    row = lax.broadcasted_iota(jnp.int32, (rows, LANES), 0)

    def final_copy(j):
        at = pl.ds(bounds[j] * LANES, (bounds[j + 1] - bounds[j]) * LANES)
        return pltpu.make_async_remote_copy(
            result.at[:, :, at],
            other.at[:, :, at],
            final_send.at[j],
            final_recv.at[j],
            {"ens": 1 - e},
            MESH,
        )

    def store_copy(which, j):
        at = pl.ds(bounds[j] * LANES, (bounds[j + 1] - bounds[j]) * LANES)
        src, slot = (result, e) if which == 0 else (other, 1 - e)
        return pltpu.make_async_copy(
            src.at[:, :, at], out.at[slot, :, :, at], store_sem.at[which, j]
        )

    for s in range(SUBSTEPS):
        src = fields.at[s % 2]
        dst = result if s == SUBSTEPS - 1 else fields.at[(s + 1) % 2]
        for j in range(CHUNKS):

            @pl.when(has_north)
            def _():
                halo_copy(s, 1, j).wait_recv()

            @pl.when(has_south)
            def _():
                halo_copy(s, 0, j).wait_recv()

            def advance(k, at):
                before = pl.ds(pl.multiple_of(lax.rem(k + tiles - 1, tiles) * LANES, LANES), LANES)
                after = pl.ds(pl.multiple_of(lax.rem(k + 1, tiles) * LANES, LANES), LANES)
                x = [src[c, :, at] for c in range(comp)]
                w, wc = wet[:, at], wcoef[:, at]
                for i in range(comp):
                    mixing = x[i]
                    for c in range(comp):
                        mixing = mixing + inter[i, c] * x[c]
                    left = jnp.where(
                        lane == 0, pltpu.roll(src[i, :, before], 1, 1), pltpu.roll(x[i], 1, 1)
                    )
                    right = jnp.where(
                        lane == LANES - 1,
                        pltpu.roll(src[i, :, after], LANES - 1, 1),
                        pltpu.roll(x[i], LANES - 1, 1),
                    )
                    up = jnp.where(row == 0, north[s, i : i + 1, at], pltpu.roll(x[i], 1, 0))
                    down = jnp.where(
                        row == rows - 1, south[s, i : i + 1, at], pltpu.roll(x[i], rows - 1, 0)
                    )
                    v = w * mixing + wc * ((up + down) + (left + right) - 4.0 * x[i])
                    dst[i, :, at] = v
                    if s < SUBSTEPS - 1:
                        send[s + 1, 0, i : i + 1, at] = v[0:1]
                        send[s + 1, 1, i : i + 1, at] = v[rows - 1 : rows]
                    elif i == 0:
                        surface[pl.ds(pl.multiple_of(k * rows, rows), rows), :] = v

            tile_loop(bounds[j], bounds[j + 1], advance)
            if s < SUBSTEPS - 1:
                send_halo(s + 1, j)
            else:
                final_copy(j).start()
                store_copy(0, j).start()

    where = loc[...]
    band_row = sum((where >= lon * i).astype(jnp.int32) for i in range(1, rows))
    column = where - band_row * lon
    tile = column // LANES
    key = tile * rows + band_row
    within = column - tile * LANES
    obs = where.shape[1]
    hot = (lax.broadcasted_iota(jnp.int32, (surface.shape[0], obs), 0) == key).astype(jnp.float32)
    picked = jnp.dot(
        surface[...].T, hot, precision=lax.Precision.HIGHEST, preferred_element_type=jnp.float32
    )
    picked = jnp.sum(
        jnp.where(lax.broadcasted_iota(jnp.int32, (LANES, obs), 0) == within, picked, 0.0),
        axis=0,
        keepdims=True,
    )
    misfit = picked - reading[...]
    partial = jnp.sum(inv_var[...] * misfit * misfit, axis=1, keepdims=True)
    pair[pl.ds(e, 1)] = jnp.broadcast_to(partial[None], (1, 8, LANES))
    pair_copy = pltpu.make_async_remote_copy(
        pair.at[e], pair.at[e], pair_sem.at[0], pair_sem.at[1], {"ens": 1 - e}, MESH
    )
    pair_copy.start()
    pair_copy.wait()
    running = pair[...]
    for r, (stride, size) in enumerate(steps):
        digit = lax.rem(me // stride, size)
        gather[r, pl.ds(digit, 1)] = running[None]
        copies = [
            pltpu.make_async_remote_copy(
                gather.at[r, digit],
                gather.at[r, digit],
                sum_send.at[r, q],
                sum_recv.at[r, q],
                {"space": dev},
                MESH,
            )
            for rr, q, _, _, dev in digit_peers()
            if rr == r
        ]
        for copy in copies:
            copy.start()
        for copy in copies:
            copy.wait()
        running = gather[r, 0]
        for q in range(1, size):
            running = running + gather[r, q]
    totals[...] = running

    for j in range(CHUNKS):
        final_copy(j).wait_recv()
        store_copy(1, j).start()
    for j in range(CHUNKS):
        final_copy(j).wait_send()
        store_copy(0, j).wait()
        store_copy(1, j).wait()
        for s in range(SUBSTEPS):

            @pl.when(has_north)
            def _():
                halo_copy(s, 0, j).wait_send()

            @pl.when(has_south)
            def _():
                halo_copy(s, 1, j).wait_send()


def body(
    peers,
    analysis,
    copy_counts,
    spreading_coefficient,
    component_interaction,
    ocean_mask,
    measured_grid_location,
    measured_surface_reading,
    measured_inverse_variance,
):
    per_slot, comp, rows, lon = analysis.shape
    slots = copy_counts.shape[0]
    tiles = -(-lon // LANES)
    wide = tiles * LANES
    deep = -(-tiles * rows // LANES) * LANES
    rounds = radix_steps(peers)
    widest = max([size for _, size in rounds] + [1])
    f32 = jnp.float32
    vmem = pl.BlockSpec(memory_space=pltpu.VMEM)
    smem = pl.BlockSpec(memory_space=pltpu.SMEM)
    hbm = pl.BlockSpec(memory_space=pl.ANY)
    dma = pltpu.SemaphoreType.DMA
    obs = measured_grid_location.shape[0]
    fields, totals = pl.pallas_call(
        functools.partial(forecast_kernel, peers),
        out_shape=(
            jax.ShapeDtypeStruct((2, comp, rows, wide), f32),
            jax.ShapeDtypeStruct((2, 8, LANES), f32),
        ),
        in_specs=[smem, smem, hbm, vmem, vmem, vmem, vmem, vmem],
        out_specs=(hbm, vmem),
        scratch_shapes=[
            pltpu.VMEM((per_slot, comp, rows, lon), f32),
            pltpu.VMEM((comp, rows, lon), f32),
            pltpu.VMEM((comp, rows, lon), f32),
            pltpu.VMEM((3, 2, comp, wide), f32),
            pltpu.VMEM((SUBSTEPS, 2, comp, wide), f32),
            pltpu.VMEM((SUBSTEPS, comp, wide), f32),
            pltpu.VMEM((SUBSTEPS, comp, wide), f32),
            pltpu.VMEM((2, comp, rows, wide), f32),
            pltpu.VMEM((comp, rows, wide), f32),
            pltpu.VMEM((comp, rows, wide), f32),
            pltpu.VMEM((rows, wide), f32),
            pltpu.VMEM((rows, wide), f32),
            pltpu.VMEM((deep, LANES), f32),
            pltpu.VMEM((2, 8, LANES), f32),
            pltpu.VMEM((max(len(rounds), 1), widest, 2, 8, LANES), f32),
            dma((per_slot,)),
            dma((2,)),
            dma((2,)),
            dma((SUBSTEPS, 2, CHUNKS)),
            dma((SUBSTEPS, 2, CHUNKS)),
            dma((CHUNKS,)),
            dma((CHUNKS,)),
            dma((2, CHUNKS)),
            dma((2,)),
            dma((max(len(rounds), 1), widest)),
            dma((max(len(rounds), 1), widest)),
        ],
        compiler_params=pltpu.CompilerParams(
            collective_id=0, has_side_effects=True, vmem_limit_bytes=48 * 1024 * 1024
        ),
        cost_estimate=pl.CostEstimate(
            flops=2 * SUBSTEPS * comp * comp * rows * lon,
            bytes_accessed=6 * comp * rows * lon * 4,
            transcendentals=0,
        ),
    )(
        copy_counts,
        component_interaction,
        analysis,
        spreading_coefficient,
        ocean_mask,
        measured_grid_location.reshape(1, obs),
        measured_surface_reading.reshape(1, obs),
        measured_inverse_variance.reshape(1, obs),
    )
    bounds = jnp.cumsum(copy_counts)
    head = jnp.min(jnp.where(bounds > 0, bounds, slots))
    position = lax.axis_index("ens") * per_slot + jnp.arange(per_slot, dtype=jnp.int32)
    from_first = position < head
    predicted = jnp.where(
        from_first[:, None, None, None], fields[0, ..., :lon][None], fields[1, ..., :lon][None]
    )
    summed = jnp.where(from_first, totals[0, 0, 0], totals[1, 0, 0])
    return predicted, -0.5 * summed / (obs * peers)


def solution(mesh):
    in_specs = (
        P(("runs", "ens"), None, "space", None),
        P("runs"),
        P(("runs", "space"), None),
        P(),
        P(("runs", "space"), None),
        P(("runs", "space")),
        P(("runs", "space")),
        P(("runs", "space")),
    )
    out_specs = (P(("runs", "ens"), None, "space", None), P(("runs", "ens")))
    return jax.shard_map(
        functools.partial(body, mesh.shape["space"]),
        mesh=mesh,
        in_specs=in_specs,
        out_specs=out_specs,
        check_vma=False,
    )
```

```python
import functools

import jax
import jax.numpy as jnp
from jax import lax
from jax.experimental import pallas as pl
from jax.experimental.pallas import tpu as pltpu
from jax.sharding import PartitionSpec as P

SUBSTEPS = 3
CHUNKS = 4
LANES = 128
GROUP = 3
MESH = pl.DeviceIdType.MESH


def radix_steps(peers):
    steps, stride = [], 1
    while peers > 1:
        size = 8 if peers % 8 == 0 else (peers if peers < 8 else 2 if peers % 2 == 0 else peers)
        steps.append((stride, size))
        stride, peers = stride * size, peers // size
    return steps


def forecast_kernel(
    peers,
    counts_hbm,
    inter_hbm,
    analysis,
    coef_hbm,
    mask_hbm,
    loc_hbm,
    reading_hbm,
    inv_var_hbm,
    out,
    score,
    counts,
    inter,
    coef,
    mask,
    loc,
    reading,
    inv_var,
    raw,
    cand,
    taken,
    edges,
    send,
    north,
    south,
    fields,
    result,
    other,
    wet,
    wcoef,
    surface,
    pair,
    gather,
    load_sem,
    edge_sem,
    cand_sem,
    send_sem,
    recv_sem,
    final_send,
    final_recv,
    pair_sem,
    sum_send,
    sum_recv,
):
    comp, rows, lon = analysis.shape[1:]
    wide = wet.shape[1]
    width = GROUP * LANES
    tiles = wide // LANES
    groups = wide // width
    slots = counts.shape[0]
    per_slot = slots // 2
    full = lon // width
    tail = lon - full * width
    half = (wide - lon) // 2
    rest = wide - lon - half
    bounds = [groups * j // CHUNKS for j in range(CHUNKS + 1)]
    steps = radix_steps(peers)

    e = lax.axis_index("ens")
    me = lax.axis_index("space")
    has_north = me > 0
    has_south = me < peers - 1

    loads = [
        pltpu.make_async_copy(analysis.at[p], raw.at[p], load_sem.at[p]) for p in range(per_slot)
    ]
    small = [
        pltpu.make_async_copy(src, dst, load_sem.at[per_slot + i])
        for i, (src, dst) in enumerate(
            (
                (counts_hbm, counts),
                (coef_hbm, coef),
                (mask_hbm, mask),
                (inter_hbm, inter),
                (loc_hbm, loc),
                (reading_hbm, reading),
                (inv_var_hbm, inv_var),
            )
        )
    ]
    for copy in small[:3] + loads + small[3:]:
        copy.start()

    def digit_peers():
        for r, (stride, size) in enumerate(steps):
            digit = lax.rem(me // stride, size)
            for q in range(1, size):
                to = lax.rem(digit + q, size)
                yield r, q, digit, to, me + (to - digit) * stride

    barrier = pltpu.get_barrier_semaphore()
    pl.semaphore_signal(barrier, inc=1, device_id={"ens": 1 - e}, device_id_type=MESH)
    waits = 1
    for r, q, digit, to, dev in digit_peers():
        pl.semaphore_signal(barrier, inc=1, device_id={"space": dev}, device_id_type=MESH)
        waits += 1

    if len(steps) > 1:

        @pl.when(has_north)
        def _():
            pl.semaphore_signal(barrier, inc=1, device_id={"space": me - 1}, device_id_type=MESH)

        @pl.when(has_south)
        def _():
            pl.semaphore_signal(barrier, inc=1, device_id={"space": me + 1}, device_id_type=MESH)

        waits = waits + has_north.astype(jnp.int32) + has_south.astype(jnp.int32)

    def tail_of(load):
        return jnp.concatenate(
            [load(lon - tail, lon), load(0, half), load(lon - rest, lon)], axis=-1
        )

    def tile_loop(first, last, body):
        def step(k, carry):
            body(k, pl.ds(pl.multiple_of(k * width, LANES), width))
            return carry

        lax.fori_loop(first, last, step, 0)

    last = pl.ds(full * width, width)

    def prepare(c, m, at):
        w = m.astype(jnp.float32)
        wet[:, at] = w
        wcoef[:, at] = w * c

    for copy in small[:3]:
        copy.wait()
    tile_loop(0, full, lambda k, at: prepare(coef[:, at], mask[:, at], at))
    prepare(
        tail_of(lambda a, b: coef[:, a:b]),
        tail_of(lambda a, b: mask[:, a:b].astype(jnp.float32)),
        last,
    )
    surface[tiles * rows :, :] = jnp.zeros((surface.shape[0] - tiles * rows, LANES), jnp.float32)

    @pl.when(jnp.logical_not(has_north))
    def _():
        for s in range(SUBSTEPS):
            north[s] = jnp.zeros(north.shape[1:], jnp.float32)

    @pl.when(jnp.logical_not(has_south))
    def _():
        for s in range(SUBSTEPS):
            south[s] = jnp.zeros(south.shape[1:], jnp.float32)

    sums, total = [], 0
    for i in range(slots):
        total = total + counts[i]
        sums.append(total)
    first = sum((v <= 0).astype(jnp.int32) for v in sums)
    final = sum((v <= slots - 1).astype(jnp.int32) for v in sums)
    mine = jnp.where(e == 0, first, final)
    theirs = jnp.where(e == 0, final, first)
    is_own = mine // per_slot == e
    their_row = theirs % per_slot
    own_row = mine % per_slot
    edge_row = jnp.where(is_own, 0, 1)

    for copy in loads:
        copy.wait()
    for copy in small[3:]:
        copy.wait()

    def pack_edges(p, slot):
        def put(load, at):
            for c in range(comp):
                v = load(c)
                edges[slot, 0, c : c + 1, at] = v[0:1]
                edges[slot, 1, c : c + 1, at] = v[rows - 1 : rows]

        tile_loop(0, full, lambda k, at: put(lambda c: raw[p, c, :, at], at))
        put(lambda c: tail_of(lambda a, b: raw[p, c, :, a:b]), last)

    pack_edges(their_row, 2)

    pl.semaphore_wait(barrier, waits)

    edge_copy = pltpu.make_async_remote_copy(
        edges.at[2], edges.at[1], edge_sem.at[0], edge_sem.at[1], {"ens": 1 - e}, MESH
    )
    edge_copy.start()
    for c in range(comp):
        cand[c] = raw[their_row, c]
    cand_copy = pltpu.make_async_remote_copy(
        cand, taken, cand_sem.at[0], cand_sem.at[1], {"ens": 1 - e}, MESH
    )
    cand_copy.start()
    pack_edges(own_row, 0)
    edge_copy.wait()

    def halo_copy(s, side, j):
        at = pl.ds(bounds[j] * width, (bounds[j + 1] - bounds[j]) * width)
        dst = south if side == 0 else north
        to = me - 1 if side == 0 else me + 1
        return pltpu.make_async_remote_copy(
            send.at[s, side, :, at],
            dst.at[s, :, at],
            send_sem.at[s, side, j],
            recv_sem.at[s, side, j],
            {"space": to},
            MESH,
        )

    def send_halo(s, j):
        @pl.when(has_north)
        def _():
            halo_copy(s, 0, j).start()

        @pl.when(has_south)
        def _():
            halo_copy(s, 1, j).start()

    for j in range(CHUNKS):

        def move(k, at):
            for side in range(2):
                send[0, side, :, at] = edges[edge_row, side, :, at]

        tile_loop(bounds[j], bounds[j + 1], move)
        send_halo(0, j)

    cand_copy.wait()

    def begin(k, at):
        for c in range(comp):
            fields[0, c, :, at] = jnp.where(is_own, raw[own_row, c, :, at], taken[c, :, at])

    tile_loop(0, full, begin)
    for c in range(comp):
        fields[0, c, :, last] = tail_of(
            lambda a, b: jnp.where(is_own, raw[own_row, c, :, a:b], taken[c, :, a:b])
        )

    lane = lax.broadcasted_iota(jnp.int32, (rows, width), 1)
    row = lax.broadcasted_iota(jnp.int32, (rows, width), 0)

    def final_copy(j):
        at = pl.ds(bounds[j] * width, (bounds[j + 1] - bounds[j]) * width)
        return pltpu.make_async_remote_copy(
            result.at[:, :, at],
            other.at[:, :, at],
            final_send.at[j],
            final_recv.at[j],
            {"ens": 1 - e},
            MESH,
        )

    for s in range(SUBSTEPS):
        src = fields.at[s % 2]
        dst = result if s == SUBSTEPS - 1 else fields.at[(s + 1) % 2]
        for j in range(CHUNKS):

            @pl.when(has_north)
            def _():
                halo_copy(s, 1, j).wait_recv()

            @pl.when(has_south)
            def _():
                halo_copy(s, 0, j).wait_recv()

            def advance(k, at):
                before = pl.ds(pl.multiple_of(lax.rem(k * GROUP + tiles - 1, tiles) * LANES, LANES), LANES)
                after = pl.ds(pl.multiple_of(lax.rem((k + 1) * GROUP, tiles) * LANES, LANES), LANES)
                x = [src[c, :, at] for c in range(comp)]
                w, wc = wet[:, at], wcoef[:, at]
                for i in range(comp):
                    mixing = x[i]
                    for c in range(comp):
                        mixing = mixing + inter[i, c] * x[c]
                    edge_l = pltpu.roll(src[i, :, before], 1, 1)
                    edge_r = pltpu.roll(src[i, :, after], LANES - 1, 1)
                    left = jnp.where(
                        lane == 0, jnp.concatenate([edge_l] * GROUP, 1), pltpu.roll(x[i], 1, 1)
                    )
                    right = jnp.where(
                        lane == width - 1,
                        jnp.concatenate([edge_r] * GROUP, 1),
                        pltpu.roll(x[i], width - 1, 1),
                    )
                    up = jnp.where(row == 0, north[s, i : i + 1, at], pltpu.roll(x[i], 1, 0))
                    down = jnp.where(
                        row == rows - 1, south[s, i : i + 1, at], pltpu.roll(x[i], rows - 1, 0)
                    )
                    v = w * mixing + wc * ((up + down) + (left + right) - 4.0 * x[i])
                    dst[i, :, at] = v
                    if s < SUBSTEPS - 1:
                        send[s + 1, 0, i : i + 1, at] = v[0:1]
                        send[s + 1, 1, i : i + 1, at] = v[rows - 1 : rows]
                    elif i == 0:
                        for g in range(GROUP):
                            to = pl.ds(pl.multiple_of((k * GROUP + g) * rows, rows), rows)
                            surface[to, :] = v[:, g * LANES : (g + 1) * LANES]

            tile_loop(bounds[j], bounds[j + 1], advance)
            if s < SUBSTEPS - 1:
                send_halo(s + 1, j)
            else:
                final_copy(j).start()

    where = loc[...]
    band_row = sum((where >= lon * i).astype(jnp.int32) for i in range(1, rows))
    column = where - band_row * lon
    tile = column // LANES
    key = tile * rows + band_row
    within = column - tile * LANES
    obs = where.shape[1]
    hot = (lax.broadcasted_iota(jnp.int32, (surface.shape[0], obs), 0) == key).astype(jnp.float32)
    picked = jnp.dot(
        surface[...].T, hot, precision=lax.Precision.HIGHEST, preferred_element_type=jnp.float32
    )
    picked = jnp.sum(
        jnp.where(lax.broadcasted_iota(jnp.int32, (LANES, obs), 0) == within, picked, 0.0),
        axis=0,
        keepdims=True,
    )
    misfit = picked - reading[...]
    partial = jnp.sum(inv_var[...] * misfit * misfit, axis=1, keepdims=True)
    pair[pl.ds(e, 1)] = jnp.broadcast_to(partial[None], (1, 8, LANES))
    pair_copy = pltpu.make_async_remote_copy(
        pair.at[e], pair.at[e], pair_sem.at[0], pair_sem.at[1], {"ens": 1 - e}, MESH
    )
    pair_copy.start()
    pair_copy.wait()
    running = pair[...]
    for r, (stride, size) in enumerate(steps):
        digit = lax.rem(me // stride, size)
        gather[r, pl.ds(digit, 1)] = running[None]
        copies = [
            pltpu.make_async_remote_copy(
                gather.at[r, digit],
                gather.at[r, digit],
                sum_send.at[r, q],
                sum_recv.at[r, q],
                {"space": dev},
                MESH,
            )
            for rr, q, _, _, dev in digit_peers()
            if rr == r
        ]
        for copy in copies:
            copy.start()
        for copy in copies:
            copy.wait()
        running = gather[r, 0]
        for q in range(1, size):
            running = running + gather[r, q]
    dup = jnp.logical_or(
        *(
            jnp.logical_and(e == slot, copied)
            for slot, copied in enumerate(
                (
                    sum((v <= 1).astype(jnp.int32) for v in sums) == first,
                    sum((v <= slots - 2).astype(jnp.int32) for v in sums) == final,
                )
            )
        )
    )
    scale = -0.5 / (obs * peers)
    x, y = running[0, 0:1, 0:2], running[1, 0:1, 0:2]
    own, far = jnp.where(e == 0, x, y), jnp.where(e == 0, y, x)
    spot = lax.broadcasted_iota(jnp.int32, (1, 2), 1)
    score[...] = scale * jnp.where(jnp.logical_or(spot == e, dup), own, far)

    def choose(at, of):
        for c in range(comp):
            a, b = result[c, :, of], other[c, :, of]
            out[e, c, :, at] = a
            out[1 - e, c, :, at] = jnp.where(dup, a, b)

    for j in range(CHUNKS):
        final_copy(j).wait_recv()
        tile_loop(bounds[j], min(bounds[j + 1], full), lambda k, at: choose(at, at))
    choose(pl.ds(full * width, tail), pl.ds(full * width, tail))
    for j in range(CHUNKS):
        final_copy(j).wait_send()
        for s in range(SUBSTEPS):

            @pl.when(has_north)
            def _():
                halo_copy(s, 0, j).wait_send()

            @pl.when(has_south)
            def _():
                halo_copy(s, 1, j).wait_send()


def body(
    peers,
    analysis,
    copy_counts,
    spreading_coefficient,
    component_interaction,
    ocean_mask,
    measured_grid_location,
    measured_surface_reading,
    measured_inverse_variance,
):
    per_slot, comp, rows, lon = analysis.shape
    slots = copy_counts.shape[0]
    width = GROUP * LANES
    wide = -(-(lon + 2 * SUBSTEPS) // width) * width
    tiles = wide // LANES
    deep = -(-tiles * rows // LANES) * LANES
    rounds = radix_steps(peers)
    widest = max([size for _, size in rounds] + [1])
    f32 = jnp.float32
    vmem = pl.BlockSpec(memory_space=pltpu.VMEM)
    hbm = pl.BlockSpec(memory_space=pltpu.HBM)
    dma = pltpu.SemaphoreType.DMA
    obs = measured_grid_location.shape[0]
    predicted, score = pl.pallas_call(
        functools.partial(forecast_kernel, peers),
        out_shape=(
            jax.ShapeDtypeStruct(analysis.shape, f32),
            jax.ShapeDtypeStruct((1, per_slot), f32),
        ),
        in_specs=[hbm] * 8,
        out_specs=(vmem, vmem),
        scratch_shapes=[
            pltpu.SMEM(copy_counts.shape, jnp.int32),
            pltpu.SMEM(component_interaction.shape, f32),
            pltpu.VMEM((rows, lon), f32),
            pltpu.VMEM((rows, lon), jnp.int32),
            pltpu.VMEM((1, obs), jnp.int32),
            pltpu.VMEM((1, obs), f32),
            pltpu.VMEM((1, obs), f32),
            pltpu.VMEM((per_slot, comp, rows, lon), f32),
            pltpu.VMEM((comp, rows, lon), f32),
            pltpu.VMEM((comp, rows, lon), f32),
            pltpu.VMEM((3, 2, comp, wide), f32),
            pltpu.VMEM((SUBSTEPS, 2, comp, wide), f32),
            pltpu.VMEM((SUBSTEPS, comp, wide), f32),
            pltpu.VMEM((SUBSTEPS, comp, wide), f32),
            pltpu.VMEM((2, comp, rows, wide), f32),
            pltpu.VMEM((comp, rows, wide), f32),
            pltpu.VMEM((comp, rows, wide), f32),
            pltpu.VMEM((rows, wide), f32),
            pltpu.VMEM((rows, wide), f32),
            pltpu.VMEM((deep, LANES), f32),
            pltpu.VMEM((2, 8, LANES), f32),
            pltpu.VMEM((max(len(rounds), 1), widest, 2, 8, LANES), f32),
            dma((per_slot + 7,)),
            dma((2,)),
            dma((2,)),
            dma((SUBSTEPS, 2, CHUNKS)),
            dma((SUBSTEPS, 2, CHUNKS)),
            dma((CHUNKS,)),
            dma((CHUNKS,)),
            dma((2,)),
            dma((max(len(rounds), 1), widest)),
            dma((max(len(rounds), 1), widest)),
        ],
        compiler_params=pltpu.CompilerParams(
            collective_id=0, has_side_effects=True, vmem_limit_bytes=64 * 1024 * 1024 - 65536
        ),
        cost_estimate=pl.CostEstimate(
            flops=2 * SUBSTEPS * comp * comp * rows * lon,
            bytes_accessed=6 * comp * rows * lon * 4,
            transcendentals=0,
        ),
    )(
        copy_counts,
        component_interaction,
        analysis,
        spreading_coefficient,
        ocean_mask,
        measured_grid_location.reshape(1, obs),
        measured_surface_reading.reshape(1, obs),
        measured_inverse_variance.reshape(1, obs),
    )
    return predicted, score.reshape(per_slot)


def solution(mesh):
    in_specs = (
        P(("runs", "ens"), None, "space", None),
        P("runs"),
        P(("runs", "space"), None),
        P(),
        P(("runs", "space"), None),
        P(("runs", "space")),
        P(("runs", "space")),
        P(("runs", "space")),
    )
    out_specs = (P(("runs", "ens"), None, "space", None), P(("runs", "ens")))
    return jax.shard_map(
        functools.partial(body, mesh.shape["space"]),
        mesh=mesh,
        in_specs=in_specs,
        out_specs=out_specs,
        check_vma=False,
    )
```

```python
import functools

import jax
import jax.numpy as jnp
from jax import lax
from jax.experimental import pallas as pl
from jax.experimental.pallas import tpu as pltpu
from jax.sharding import PartitionSpec as P

SUBSTEPS = 3
CHUNKS = 4
LANES = 128
GROUP = 3
MESH = pl.DeviceIdType.MESH


def radix_steps(peers):
    steps, stride = [], 1
    while peers > 1:
        size = 8 if peers % 8 == 0 else (peers if peers < 8 else 2 if peers % 2 == 0 else peers)
        steps.append((stride, size))
        stride, peers = stride * size, peers // size
    return steps


def forecast_kernel(
    peers,
    counts_hbm,
    inter_hbm,
    analysis,
    coef_hbm,
    mask_hbm,
    loc_hbm,
    reading_hbm,
    inv_var_hbm,
    out,
    score,
    counts,
    inter,
    coef,
    mask,
    loc,
    reading,
    inv_var,
    raw,
    cand,
    taken,
    edges,
    send,
    north,
    south,
    fields_a,
    fields_b,
    kmat,
    result,
    other,
    wet,
    wcoef,
    surface,
    pair,
    gather,
    load_sem,
    edge_sem,
    cand_sem,
    send_sem,
    recv_sem,
    final_send,
    final_recv,
    pair_sem,
    sum_send,
    sum_recv,
):
    comp, rows, lon = analysis.shape[1:]
    wide = wet.shape[1]
    width = GROUP * LANES
    tiles = wide // LANES
    groups = wide // width
    slots = counts.shape[0]
    per_slot = slots // 2
    full = lon // width
    tail = lon - full * width
    ring = -(-(lon + 2 * SUBSTEPS) // LANES) * LANES
    half = (ring - lon) // 2
    rest = ring - lon - half
    bounds = [groups * j // CHUNKS for j in range(CHUNKS + 1)]
    steps = radix_steps(peers)

    e = lax.axis_index("ens")
    me = lax.axis_index("space")
    has_north = me > 0
    has_south = me < peers - 1

    loads = [
        pltpu.make_async_copy(analysis.at[p], raw.at[p], load_sem.at[p]) for p in range(per_slot)
    ]
    small = [
        pltpu.make_async_copy(src, dst, load_sem.at[per_slot + i])
        for i, (src, dst) in enumerate(
            (
                (counts_hbm, counts),
                (coef_hbm, coef),
                (mask_hbm, mask),
                (inter_hbm, inter),
                (loc_hbm, loc),
                (reading_hbm, reading),
                (inv_var_hbm, inv_var),
            )
        )
    ]
    for copy in small[:3] + loads + small[3:]:
        copy.start()

    def digit_peers():
        for r, (stride, size) in enumerate(steps):
            digit = lax.rem(me // stride, size)
            for q in range(1, size):
                to = lax.rem(digit + q, size)
                yield r, q, digit, to, me + (to - digit) * stride

    barrier = pltpu.get_barrier_semaphore()
    pl.semaphore_signal(barrier, inc=1, device_id={"ens": 1 - e}, device_id_type=MESH)
    waits = 1
    for r, q, digit, to, dev in digit_peers():
        pl.semaphore_signal(barrier, inc=1, device_id={"space": dev}, device_id_type=MESH)
        waits += 1

    if len(steps) > 1:

        @pl.when(has_north)
        def _():
            pl.semaphore_signal(barrier, inc=1, device_id={"space": me - 1}, device_id_type=MESH)

        @pl.when(has_south)
        def _():
            pl.semaphore_signal(barrier, inc=1, device_id={"space": me + 1}, device_id_type=MESH)

        waits = waits + has_north.astype(jnp.int32) + has_south.astype(jnp.int32)

    def tail_of(load):
        return jnp.concatenate(
            [load(lon - tail, lon), load(0, half), load(lon - rest, lon), load(0, wide - ring)][: 3 + (wide > ring)], axis=-1
        )

    def tile_loop(first, last, body):
        def step(k, carry):
            body(k, pl.ds(pl.multiple_of(k * width, LANES), width))
            return carry

        lax.fori_loop(first, last, step, 0)

    last = pl.ds(full * width, width)

    def prepare(c, m, at):
        w = m.astype(jnp.float32)
        wet[:, at] = w
        wcoef[:, at] = w * c

    for copy in small[:3]:
        copy.wait()
    tile_loop(0, full, lambda k, at: prepare(coef[:, at], mask[:, at], at))
    prepare(
        tail_of(lambda a, b: coef[:, a:b]),
        tail_of(lambda a, b: mask[:, a:b].astype(jnp.float32)),
        last,
    )
    surface[tiles * rows :, :] = jnp.zeros((surface.shape[0] - tiles * rows, LANES), jnp.float32)

    if wide > ring:
        for s in range(SUBSTEPS):
            north[s, :, ring:] = jnp.zeros((comp, wide - ring), jnp.float32)
            south[s, :, ring:] = jnp.zeros((comp, wide - ring), jnp.float32)

    @pl.when(jnp.logical_not(has_north))
    def _():
        for s in range(SUBSTEPS):
            north[s] = jnp.zeros(north.shape[1:], jnp.float32)

    @pl.when(jnp.logical_not(has_south))
    def _():
        for s in range(SUBSTEPS):
            south[s] = jnp.zeros(south.shape[1:], jnp.float32)

    sums, total = [], 0
    for i in range(slots):
        total = total + counts[i]
        sums.append(total)
    first = sum((v <= 0).astype(jnp.int32) for v in sums)
    final = sum((v <= slots - 1).astype(jnp.int32) for v in sums)
    mine = jnp.where(e == 0, first, final)
    theirs = jnp.where(e == 0, final, first)
    is_own = mine // per_slot == e
    their_row = theirs % per_slot
    own_row = mine % per_slot
    edge_row = jnp.where(is_own, 0, 1)

    for copy in loads:
        copy.wait()
    for copy in small[3:]:
        copy.wait()

    size = comp * rows
    across = lax.broadcasted_iota(jnp.int32, (rows, size), 1)
    down_row = lax.broadcasted_iota(jnp.int32, (rows, size), 0)
    blocks = []
    for i in range(comp):
        block = jnp.zeros((rows, size), jnp.float32)
        for c in range(comp):
            block = jnp.where(across == c * rows + down_row, inter[i, c], block)
        blocks.append(block)
    coupling = jnp.concatenate(blocks, 0)
    high = coupling.astype(jnp.bfloat16)
    low = (coupling - high.astype(jnp.float32)).astype(jnp.bfloat16)
    kmat[...] = jnp.concatenate([high, high, low], 1)

    def pack_edges(p, slot):
        def put(load, at):
            for c in range(comp):
                v = load(c)
                edges[slot, 0, c : c + 1, at] = v[0:1]
                edges[slot, 1, c : c + 1, at] = v[rows - 1 : rows]

        tile_loop(0, full, lambda k, at: put(lambda c: raw[p, c, :, at], at))
        put(lambda c: tail_of(lambda a, b: raw[p, c, :, a:b]), last)

    pack_edges(their_row, 2)

    pl.semaphore_wait(barrier, waits)

    edge_copy = pltpu.make_async_remote_copy(
        edges.at[2], edges.at[1], edge_sem.at[0], edge_sem.at[1], {"ens": 1 - e}, MESH
    )
    edge_copy.start()
    for c in range(comp):
        cand[c] = raw[their_row, c]
    cand_copy = pltpu.make_async_remote_copy(
        cand, taken, cand_sem.at[0], cand_sem.at[1], {"ens": 1 - e}, MESH
    )
    cand_copy.start()
    pack_edges(own_row, 0)
    edge_copy.wait()

    def halo_copy(s, side, j):
        at = pl.ds(bounds[j] * width, min(bounds[j + 1] * width, ring) - bounds[j] * width)
        dst = south if side == 0 else north
        to = me - 1 if side == 0 else me + 1
        return pltpu.make_async_remote_copy(
            send.at[s, side, :, at],
            dst.at[s, :, at],
            send_sem.at[s, side, j],
            recv_sem.at[s, side, j],
            {"space": to},
            MESH,
        )

    def send_halo(s, j):
        @pl.when(has_north)
        def _():
            halo_copy(s, 0, j).start()

        @pl.when(has_south)
        def _():
            halo_copy(s, 1, j).start()

    for j in range(CHUNKS):

        def move(k, at):
            for side in range(2):
                send[0, side, :, at] = edges[edge_row, side, :, at]

        tile_loop(bounds[j], bounds[j + 1], move)
        send_halo(0, j)

    cand_copy.wait()

    def begin(k, at):
        for c in range(comp):
            fields_a[c, :, at] = jnp.where(is_own, raw[own_row, c, :, at], taken[c, :, at])

    tile_loop(0, full, begin)
    for c in range(comp):
        fields_a[c, :, last] = tail_of(
            lambda a, b: jnp.where(is_own, raw[own_row, c, :, a:b], taken[c, :, a:b])
        )

    lane = lax.broadcasted_iota(jnp.int32, (rows, width), 1)
    row = lax.broadcasted_iota(jnp.int32, (rows, width), 0)

    def final_copy(j):
        at = pl.ds(bounds[j] * width, (bounds[j + 1] - bounds[j]) * width)
        return pltpu.make_async_remote_copy(
            result.at[:, :, at],
            other.at[:, :, at],
            final_send.at[j],
            final_recv.at[j],
            {"ens": 1 - e},
            MESH,
        )

    for s in range(SUBSTEPS):
        src = (fields_a, fields_b)[s % 2]
        dst = result if s == SUBSTEPS - 1 else (fields_a, fields_b)[(s + 1) % 2]
        for j in range(CHUNKS):

            @pl.when(has_north)
            def _():
                halo_copy(s, 1, j).wait_recv()

            @pl.when(has_south)
            def _():
                halo_copy(s, 0, j).wait_recv()

            def advance(k, at):
                before = pl.ds(pl.multiple_of(lax.rem(k * GROUP + ring // LANES - 1, ring // LANES) * LANES, LANES), LANES)
                after = pl.ds(pl.multiple_of(lax.rem((k + 1) * GROUP, tiles) * LANES, LANES), LANES)
                x = [src[c, :, at] for c in range(comp)]
                w, wc = wet[:, at], wcoef[:, at]
                flat = jnp.concatenate(x, 0)
                high = flat.astype(jnp.bfloat16)
                low = (flat - high.astype(jnp.float32)).astype(jnp.bfloat16)
                mixed = jnp.dot(
                    kmat[...],
                    jnp.concatenate([high, low, high], 0),
                    preferred_element_type=jnp.float32,
                )
                done = []
                for i in range(comp):
                    mixing = x[i] + mixed[i * rows : (i + 1) * rows]
                    edge_l = pltpu.roll(src[i, :, before], 1, 1)
                    edge_r = pltpu.roll(src[i, :, after], LANES - 1, 1)
                    left = jnp.where(
                        lane == 0, jnp.concatenate([edge_l] * GROUP, 1), pltpu.roll(x[i], 1, 1)
                    )
                    right = jnp.where(
                        lane == width - 1,
                        jnp.concatenate([edge_r] * GROUP, 1),
                        pltpu.roll(x[i], width - 1, 1),
                    )
                    up = jnp.where(row == 0, north[s, i : i + 1, at], pltpu.roll(x[i], 1, 0))
                    down = jnp.where(
                        row == rows - 1, south[s, i : i + 1, at], pltpu.roll(x[i], rows - 1, 0)
                    )
                    done.append(w * mixing + wc * ((up + down) + (left + right) - 4.0 * x[i]))
                for i, v in enumerate(done):
                    dst[i, :, at] = v
                    if s < SUBSTEPS - 1:
                        send[s + 1, 0, i : i + 1, at] = v[0:1]
                        send[s + 1, 1, i : i + 1, at] = v[rows - 1 : rows]
                    elif i == 0:
                        for g in range(GROUP):
                            to = pl.ds(pl.multiple_of((k * GROUP + g) * rows, rows), rows)
                            surface[to, :] = v[:, g * LANES : (g + 1) * LANES]

            tile_loop(bounds[j], bounds[j + 1], advance)
            if s < SUBSTEPS - 1:
                send_halo(s + 1, j)
            else:
                final_copy(j).start()

    where = loc[...]
    band_row = sum((where >= lon * i).astype(jnp.int32) for i in range(1, rows))
    column = where - band_row * lon
    tile = column // LANES
    key = tile * rows + band_row
    within = column - tile * LANES
    obs = where.shape[1]
    hot = (lax.broadcasted_iota(jnp.int32, (surface.shape[0], obs), 0) == key).astype(jnp.float32)
    picked = jnp.dot(
        surface[...].T, hot, precision=lax.Precision.HIGHEST, preferred_element_type=jnp.float32
    )
    picked = jnp.sum(
        jnp.where(lax.broadcasted_iota(jnp.int32, (LANES, obs), 0) == within, picked, 0.0),
        axis=0,
        keepdims=True,
    )
    misfit = picked - reading[...]
    partial = jnp.sum(inv_var[...] * misfit * misfit, axis=1, keepdims=True)
    pair[pl.ds(e, 1)] = jnp.broadcast_to(partial[None], (1, 8, LANES))
    pair_copy = pltpu.make_async_remote_copy(
        pair.at[e], pair.at[e], pair_sem.at[0], pair_sem.at[1], {"ens": 1 - e}, MESH
    )
    dup = jnp.logical_or(
        *(
            jnp.logical_and(e == slot, copied)
            for slot, copied in enumerate(
                (
                    sum((v <= 1).astype(jnp.int32) for v in sums) == first,
                    sum((v <= slots - 2).astype(jnp.int32) for v in sums) == final,
                )
            )
        )
    )
    def choose(at, of):
        for c in range(comp):
            a, b = result[c, :, of], other[c, :, of]
            out[e, c, :, at] = a
            out[1 - e, c, :, at] = jnp.where(dup, a, b)

    def finish(chunks):
        for j in chunks:
            final_copy(j).wait_recv()
            tile_loop(bounds[j], min(bounds[j + 1], full), lambda k, at: choose(at, at))

    pair_copy.start()
    finish(range(CHUNKS - 1))
    pair_copy.wait()
    running = pair[...]
    for r, (stride, size) in enumerate(steps):
        digit = lax.rem(me // stride, size)
        gather[r, pl.ds(digit, 1)] = running[None]
        copies = [
            pltpu.make_async_remote_copy(
                gather.at[r, digit],
                gather.at[r, digit],
                sum_send.at[r, q],
                sum_recv.at[r, q],
                {"space": dev},
                MESH,
            )
            for rr, q, _, _, dev in digit_peers()
            if rr == r
        ]
        for copy in copies:
            copy.start()
        if r == 0:
            finish([CHUNKS - 1])
            choose(pl.ds(full * width, tail), pl.ds(full * width, tail))
        for copy in copies:
            copy.wait()
        running = gather[r, 0]
        for q in range(1, size):
            running = running + gather[r, q]
    scale = -0.5 / (obs * peers)
    x, y = running[0, 0:1, 0:2], running[1, 0:1, 0:2]
    own, far = jnp.where(e == 0, x, y), jnp.where(e == 0, y, x)
    spot = lax.broadcasted_iota(jnp.int32, (1, 2), 1)
    score[...] = scale * jnp.where(jnp.logical_or(spot == e, dup), own, far)

    for j in range(CHUNKS):
        final_copy(j).wait_send()
        for s in range(SUBSTEPS):

            @pl.when(has_north)
            def _():
                halo_copy(s, 0, j).wait_send()

            @pl.when(has_south)
            def _():
                halo_copy(s, 1, j).wait_send()


def body(
    peers,
    analysis,
    copy_counts,
    spreading_coefficient,
    component_interaction,
    ocean_mask,
    measured_grid_location,
    measured_surface_reading,
    measured_inverse_variance,
):
    per_slot, comp, rows, lon = analysis.shape
    slots = copy_counts.shape[0]
    width = GROUP * LANES
    wide = -(-(lon + 2 * SUBSTEPS) // width) * width
    tiles = wide // LANES
    deep = -(-tiles * rows // LANES) * LANES
    rounds = radix_steps(peers)
    widest = max([size for _, size in rounds] + [1])
    f32 = jnp.float32
    vmem = pl.BlockSpec(memory_space=pltpu.VMEM)
    hbm = pl.BlockSpec(memory_space=pltpu.HBM)
    dma = pltpu.SemaphoreType.DMA
    obs = measured_grid_location.shape[0]
    predicted, score = pl.pallas_call(
        functools.partial(forecast_kernel, peers),
        out_shape=(
            jax.ShapeDtypeStruct(analysis.shape, f32),
            jax.ShapeDtypeStruct((1, per_slot), f32),
        ),
        in_specs=[hbm] * 8,
        out_specs=(vmem, vmem),
        scratch_shapes=[
            pltpu.SMEM(copy_counts.shape, jnp.int32),
            pltpu.SMEM(component_interaction.shape, f32),
            pltpu.VMEM((rows, lon), f32),
            pltpu.VMEM((rows, lon), jnp.int32),
            pltpu.VMEM((1, obs), jnp.int32),
            pltpu.VMEM((1, obs), f32),
            pltpu.VMEM((1, obs), f32),
            pltpu.VMEM((per_slot, comp, rows, lon), f32),
            pltpu.VMEM((comp, rows, lon), f32),
            pltpu.VMEM((comp, rows, lon), f32),
            pltpu.VMEM((3, 2, comp, wide), f32),
            pltpu.VMEM((SUBSTEPS, 2, comp, wide), f32),
            pltpu.VMEM((SUBSTEPS, comp, wide), f32),
            pltpu.VMEM((SUBSTEPS, comp, wide), f32),
            pltpu.VMEM((comp, rows, wide), f32),
            pltpu.VMEM((comp, rows, wide), f32),
            pltpu.VMEM((comp * rows, 3 * comp * rows), jnp.bfloat16),
            pltpu.VMEM((comp, rows, wide), f32),
            pltpu.VMEM((comp, rows, wide), f32),
            pltpu.VMEM((rows, wide), f32),
            pltpu.VMEM((rows, wide), f32),
            pltpu.VMEM((deep, LANES), f32),
            pltpu.VMEM((2, 8, LANES), f32),
            pltpu.VMEM((max(len(rounds), 1), widest, 2, 8, LANES), f32),
            dma((per_slot + 7,)),
            dma((2,)),
            dma((2,)),
            dma((SUBSTEPS, 2, CHUNKS)),
            dma((SUBSTEPS, 2, CHUNKS)),
            dma((CHUNKS,)),
            dma((CHUNKS,)),
            dma((2,)),
            dma((max(len(rounds), 1), widest)),
            dma((max(len(rounds), 1), widest)),
        ],
        compiler_params=pltpu.CompilerParams(
            collective_id=0, has_side_effects=True, vmem_limit_bytes=64 * 1024 * 1024 - 65536
        ),
        cost_estimate=pl.CostEstimate(
            flops=2 * SUBSTEPS * comp * comp * rows * lon,
            bytes_accessed=6 * comp * rows * lon * 4,
            transcendentals=0,
        ),
    )(
        copy_counts,
        component_interaction,
        analysis,
        spreading_coefficient,
        ocean_mask,
        measured_grid_location.reshape(1, obs),
        measured_surface_reading.reshape(1, obs),
        measured_inverse_variance.reshape(1, obs),
    )
    return predicted, score.reshape(per_slot)


def solution(mesh):
    in_specs = (
        P(("runs", "ens"), None, "space", None),
        P("runs"),
        P(("runs", "space"), None),
        P(),
        P(("runs", "space"), None),
        P(("runs", "space")),
        P(("runs", "space")),
        P(("runs", "space")),
    )
    out_specs = (P(("runs", "ens"), None, "space", None), P(("runs", "ens")))
    return jax.shard_map(
        functools.partial(body, mesh.shape["space"]),
        mesh=mesh,
        in_specs=in_specs,
        out_specs=out_specs,
        check_vma=False,
    )
```
